512 devices in a mesh: ta: 16 (over z), aa: 32 (over y, x, core).
Axes of the slice: x: 4, y: 4, z: 16, core: 2. Of those that a mesh axis runs over, the one named last changes fastest.
Arguments:
- voltages: float32 [6144, 2, 2, 4096], P('ta', None, None, 'aa'), may hold values from -6 to 6
- taps: float32 [4, 16], replicated, may hold values from -3 to 3
- tile_map: int32 [32, 17], P('aa'), may hold values from 0 to 16, each once within a row
Outputs:
- visibilities: float32 [544, 32, 2, 128, 128], P('aa', 'ta')
The draws below stay inside these ranges and needn't reach their ends.
Inputs may be any that keep to these rules, and one draw needn't show every extreme that they name: `tile_map`: each row holds every number 0 to 16 exactly once.
All inputs are finite; a program needn't handle non-finite values.
Results may differ from the reference program's by a relative error of at most 0.0003.
Values sent between devices are 32-bit elements; how exact they have to be, the bound alone decides.
No kernel may reach another device: no remote copies, remote signals or barrier semaphores. Data moves between devices by JAX's collectives and lax.ppermute only.
A program may use at most 128 MiB of HBM per device.

```python
import math
import jax
import jax.numpy as jnp
from jax import lax

ANTENNA_BLOCK = 64
SPEC_DEV = 24
TAPS = 4
FINE = 16
COARSE = 2
INPUTS = 4096
SAMPLES = 6144
SLOTS = 17
N_TA = 16
N_AA = 32


def block_scale(stream_key, extent, pieces, smallest, largest):
    def one(dim, shards_of):
        draws = jax.random.uniform(jax.random.fold_in(jax.random.fold_in(stream_key, 6), dim), (shards_of,), jnp.float32, smallest / len(pieces), largest / len(pieces))
        return jnp.repeat(jnp.exp(draws), extent[dim] // shards_of).reshape((-1,) + (1,) * (len(extent) - dim - 1))

    loudness = one(*pieces[0])
    for cut in pieces[1:]:
        loudness = loudness * one(*cut)
    return loudness


def bell_draw(own_key, dims, spread, reach, split=(), kind=jnp.bfloat16):
    array = jax.random.normal(own_key, dims, jnp.float32) * spread
    if len(split) > 0:
        array = block_scale(own_key, dims, split, -0.22, 0.18) * array
    return jnp.clip(array, min=-reach, max=reach).astype(kind)


def setup_inputs(seed: int = 0) -> dict:
    seeds = jax.random.split(jax.random.key(seed), 4)
    voltages = bell_draw(seeds[0], (SAMPLES, COARSE, 2, INPUTS), 1.0, 6.0, ((0, 16), (3, 32)), jnp.float32)
    taps = bell_draw(seeds[1], (TAPS, FINE), TAPS ** -0.5, 3.0, (), jnp.float32)
    tile_map = jax.vmap(lambda own: jax.random.permutation(own, SLOTS))(jax.random.split(seeds[2], N_AA)).reshape((N_AA, SLOTS)).astype(jnp.int32)
    return {"voltages": voltages, "taps": taps, "tile_map": tile_map}


def transform(summed):
    count = summed.shape[1]
    steps = jnp.arange(count, dtype=jnp.int32)
    phase = steps[:, None] * steps[None, :] % count
    theta = phase.astype(jnp.float32) * (2.0 * math.pi / count)
    cosine = jnp.cos(theta)
    sine = jnp.sin(theta)
    scale = 1.0 / math.sqrt(count)
    highest = lax.Precision.HIGHEST
    real_in = summed[:, :, :, 0]
    imag_in = summed[:, :, :, 1]
    real_out = (jnp.einsum('mjcb,jf->mcfb', real_in, cosine, precision=highest) + jnp.einsum('mjcb,jf->mcfb', imag_in, sine, precision=highest)) * scale
    imag_out = (jnp.einsum('mjcb,jf->mcfb', imag_in, cosine, precision=highest) - jnp.einsum('mjcb,jf->mcfb', real_in, sine, precision=highest)) * scale
    stacked = jnp.stack([real_out, imag_out], axis=3)
    array_shape = stacked.shape
    return stacked.reshape(array_shape[0], array_shape[1] * array_shape[2], 2, array_shape[4])

def correlate(left_block, right_block, total):
    highest = lax.Precision.HIGHEST
    left_real = left_block[:, :, 0]
    left_imag = left_block[:, :, 1]
    right_real = right_block[:, :, 0]
    right_imag = right_block[:, :, 1]
    real_part = jnp.einsum('tci,tcj->cij', left_real, right_real, precision=highest) + jnp.einsum('tci,tcj->cij', left_imag, right_imag, precision=highest)
    imag_part = jnp.einsum('tci,tcj->cij', left_imag, right_real, precision=highest) - jnp.einsum('tci,tcj->cij', left_real, right_imag, precision=highest)
    return jnp.stack([real_part, imag_part], axis=1) / total

def reference(voltages, taps, tile_map):
    nspec = SPEC_DEV * N_TA
    block_width = 2 * ANTENNA_BLOCK
    lead = (TAPS - 1) * FINE
    padded = jnp.concatenate([jnp.zeros((lead,) + voltages.shape[1:], jnp.float32), voltages], axis=0)
    framed = padded.reshape(nspec + TAPS - 1, FINE, COARSE, 2, voltages.shape[3])
    filtered = jnp.zeros((nspec, FINE, COARSE, 2, voltages.shape[3]), jnp.float32)
    for tap in range(TAPS):
        first = TAPS - 1 - tap
        filtered = filtered + taps[tap][None, :, None, None, None] * framed[first:first + nspec]
    spectra = transform(filtered)

    def one_slot(index):
        block = index // SLOTS
        place = index % SLOTS
        distance = tile_map[block, place]
        partner = (block + distance) % N_AA
        left_block = lax.dynamic_slice_in_dim(spectra, (block * block_width).astype(jnp.int32), block_width, 3)
        right_block = lax.dynamic_slice_in_dim(spectra, (partner * block_width).astype(jnp.int32), block_width, 3)
        return correlate(left_block, right_block, float(nspec))
    return lax.map(one_slot, jnp.arange(N_AA * SLOTS, dtype=jnp.int32))
```

```python
import functools
import math

import jax
import jax.numpy as jnp
import numpy as np
from jax import lax
from jax.experimental import pallas as pl
from jax.experimental.pallas import tpu as pltpu
from jax.sharding import PartitionSpec as P

TAPS = 4
FINE = 16
COARSE = 2
NX = 4
CHIPS = 16
PAIRS = CHIPS // 2 + 1


def dft_rows(frames):
    groups = COARSE * FINE // 2
    w = np.zeros((2, 2, groups, frames, frames, FINE, COARSE, 2), np.float64)
    j = np.arange(FINE)
    for k in range(2):
        for g in range(groups):
            c, f = g // (FINE // 2), 2 * (g % (FINE // 2)) + k
            theta = 2.0 * math.pi * ((j * f) % FINE) / FINE
            cosine, sine = np.cos(theta) / math.sqrt(FINE), np.sin(theta) / math.sqrt(FINE)
            for m in range(frames):
                w[k, 0, g, m, m, :, c, 0] = cosine
                w[k, 0, g, m, m, :, c, 1] = sine
                w[k, 1, g, m, m, :, c, 0] = -sine
                w[k, 1, g, m, m, :, c, 1] = cosine
    return w.reshape(2, 2, groups * frames, frames * FINE * COARSE * 2).astype(np.float32)


def spectra_kernel(k_ref, own_ref, other_ref, own_lead_ref, other_lead_ref, taps_ref, w_ref, out_ref, pad):
    first = k_ref[0] == 0
    lead = own_lead_ref.shape[0]
    lanes = own_ref.shape[1]
    for source, mate, rows in (
        (own_lead_ref, other_lead_ref, pl.ds(0, lead)),
        (own_ref, other_ref, pl.ds(lead, own_ref.shape[0])),
    ):
        a, b = source[...], mate[...]
        pad[rows, 0:lanes] = jnp.where(first, a, b)
        pad[rows, lanes : 2 * lanes] = jnp.where(first, b, a)
    frame = taps_ref.shape[1]
    chunk = w_ref.shape[3]
    per = chunk // frame
    groups = out_ref.shape[0]
    tap_rows = [jnp.concatenate([taps_ref[p], taps_ref[p]], axis=1)[None] for p in range(TAPS)]
    for part in range(own_ref.shape[0] // chunk):
        total = None
        for p in range(TAPS):
            rows = pad[pl.ds(part * chunk + (TAPS - 1 - p) * frame, chunk), :]
            term = tap_rows[p] * rows.reshape(per, frame, 2 * lanes)
            total = term if total is None else total + term
        total = total.reshape(chunk, 2 * lanes)
        for ri in range(2):
            result = jnp.dot(
                w_ref[0, ri], total, precision=lax.Precision.HIGHEST, preferred_element_type=jnp.float32
            )
            out_ref[:, pl.ds(part * per, per), pl.ds(ri * 2 * lanes, 2 * lanes)] = result.reshape(
                groups, per, 2 * lanes
            )


def spectra_of(k, own, other, own_lead, other_lead, taps):
    frames = 8
    rows, lanes = own.shape
    w = jnp.asarray(dft_rows(frames))
    tap_rows = jnp.broadcast_to(jnp.repeat(taps, COARSE * 2, axis=1)[:, :, None], (TAPS, FINE * COARSE * 2, lanes))
    groups = COARSE * FINE // 2
    whole = lambda shape: pl.BlockSpec(shape, lambda i, k: (0,) * len(shape))
    return pl.pallas_call(
        spectra_kernel,
        out_shape=jax.ShapeDtypeStruct((groups, rows // (FINE * COARSE * 2), 4 * lanes), jnp.float32),
        grid_spec=pltpu.PrefetchScalarGridSpec(
            num_scalar_prefetch=1,
            grid=(1,),
            in_specs=[
                whole(own.shape),
                whole(other.shape),
                whole(own_lead.shape),
                whole(other_lead.shape),
                whole(tap_rows.shape),
                pl.BlockSpec((1,) + w.shape[1:], lambda i, k: (k[0], 0, 0, 0)),
            ],
            out_specs=whole((groups, rows // (FINE * COARSE * 2), 4 * lanes)),
            scratch_shapes=[pltpu.VMEM((rows + own_lead.shape[0], 2 * lanes), jnp.float32)],
        ),
        compiler_params=pltpu.CompilerParams(vmem_limit_bytes=32 * 2**20),
    )(k, own, other, own_lead, other_lead, tap_rows, w)


def split(x):
    high = x.astype(jnp.bfloat16)
    return high, (x - high.astype(jnp.float32)).astype(jnp.bfloat16)


def correlate_kernel(scale, at_ref, left_ref, right_ref, own_ref, send_ref, left_high, left_low):
    width = left_ref.shape[1] // 2
    half = width // 2
    total = left_ref.shape[0]

    @pl.when(pl.program_id(0) == 0)
    def _():
        turned = left_ref[...].T
        real_high, real_low = split(turned[:width] * scale)
        imag_high, imag_low = split(turned[width:] * scale)
        for store, real, imag in ((left_high, real_high, imag_high), (left_low, real_low, imag_low)):
            store[0:width, 0:total] = real
            store[0:width, total : 2 * total] = imag
            store[width : 2 * width, 0:total] = imag
            store[width : 2 * width, total : 2 * total] = -real

    right = right_ref[0]
    high, low = split(jnp.concatenate([right[:, :width], right[:, width:]], axis=0))
    dot = functools.partial(jnp.dot, preferred_element_type=jnp.float32)
    product = dot(left_high[...], high) + dot(left_high[...], low) + dot(left_low[...], high)
    first = at_ref[0] == 0

    for mine, goal in ((True, own_ref), (False, send_ref)):
        for r in range(2):
            for ri in range(2):
                rows0 = product[ri * width : ri * width + half, r * half : (r + 1) * half]
                rows1 = product[ri * width + half : (ri + 1) * width, r * half : (r + 1) * half]
                goal[r, ri] = jnp.where(first, rows0, rows1) if mine else jnp.where(first, rows1, rows0)


def correlated(at, left, rights, spectra_count):
    rows, lanes = left.shape
    half = lanes // 4
    tiles = jax.ShapeDtypeStruct((2 * PAIRS, 2, half, half), jnp.float32)
    return pl.pallas_call(
        functools.partial(correlate_kernel, 1.0 / spectra_count),
        out_shape=(tiles, tiles),
        grid_spec=pltpu.PrefetchScalarGridSpec(
            num_scalar_prefetch=1,
            grid=(PAIRS,),
            in_specs=[
                pl.BlockSpec((rows, lanes), lambda e, at: (0, 0)),
                pl.BlockSpec((1, rows, lanes), lambda e, at: (lax.rem(at[1] + e, CHIPS), 0, 0)),
            ],
            out_specs=[pl.BlockSpec((2, 2, half, half), lambda e, at: (e, 0, 0, 0))] * 2,
            scratch_shapes=[pltpu.VMEM((lanes, 2 * rows), jnp.bfloat16)] * 2,
        ),
        compiler_params=pltpu.CompilerParams(vmem_limit_bytes=40 * 2**20),
    )(at, left, rights)


def place_kernel(at_ref, map_ref, own_ref, got_ref, out_ref, sems):
    k = at_ref[0]
    slots = out_ref.shape[0]
    copies = []
    for s in range(slots):
        tile = map_ref[s] + k
        copies.append(pltpu.make_async_copy(own_ref.at[tile], out_ref.at[s, k], sems.at[2 * s]))
        copies.append(pltpu.make_async_copy(got_ref.at[tile], out_ref.at[s, 1 - k], sems.at[2 * s + 1]))
    for copy in copies:
        copy.start()
    for copy in copies:
        copy.wait()


def placed(at, slot_row, own, got):
    slots = slot_row.shape[0]
    half = own.shape[-1]
    return pl.pallas_call(
        place_kernel,
        out_shape=jax.ShapeDtypeStruct((slots, 2, 2, half, half), jnp.float32),
        grid_spec=pltpu.PrefetchScalarGridSpec(
            num_scalar_prefetch=2,
            grid=(1,),
            in_specs=[pl.BlockSpec(memory_space=pl.ANY)] * 2,
            out_specs=pl.BlockSpec(memory_space=pl.ANY),
            scratch_shapes=[pltpu.SemaphoreType.DMA((2 * slots,))],
        ),
    )(at, slot_row, own, got)


def local(voltages, taps, tile_map):
    n_ta, n_aa = lax.axis_size("ta"), lax.axis_size("aa")
    me = lax.axis_index("aa").astype(jnp.int32)
    k = lax.rem(me, 2)
    at = jnp.stack([k, me // 2])
    samples, coarse, parts, lanes = voltages.shape
    own = voltages.reshape(samples * coarse * parts, lanes)
    lead = own[own.shape[0] - (TAPS - 1) * FINE * coarse * parts :]
    mate = [(i, i ^ 1) for i in range(n_aa)]
    other = lax.ppermute(own, "aa", mate)
    own_lead = lax.ppermute(lead, "ta", [(t, t + 1) for t in range(n_ta - 1)])
    other_lead = lax.ppermute(own_lead, "aa", mate)
    spectra = spectra_of(at, own, other, own_lead, other_lead, taps)
    block = lax.all_to_all(spectra, "ta", split_axis=0, concat_axis=0, tiled=True)
    block = block.reshape(-1, 4 * lanes)
    same_core = [[2 * c + core for c in range(n_aa // 2)] for core in range(2)]
    gathered = lax.all_gather(block, "aa", axis_index_groups=same_core)
    own_tiles, send_tiles = correlated(at, block, gathered, block.shape[0])
    got_tiles = lax.ppermute(send_tiles, "aa", mate)
    return placed(at, tile_map[0], own_tiles, got_tiles)


def solution(mesh):
    in_specs = (P("ta", None, None, "aa"), P(), P("aa", None))
    out_specs = P("aa", "ta", None, None, None)
    return jax.shard_map(local, mesh=mesh, in_specs=in_specs, out_specs=out_specs, check_vma=False)
```

```python
import functools
import math

import jax
import jax.numpy as jnp
import numpy as np
from jax import lax
from jax.experimental import pallas as pl
from jax.experimental.pallas import tpu as pltpu
from jax.sharding import PartitionSpec as P

TAPS = 4
FINE = 16
COARSE = 2
NY = 4
NX = 4


def dft_rows(frames):
    groups = COARSE * FINE // 2
    w = np.zeros((2, 2, groups, frames, frames, FINE, COARSE, 2), np.float64)
    j = np.arange(FINE)
    for k in range(2):
        for g in range(groups):
            c, f = g // (FINE // 2), 2 * (g % (FINE // 2)) + k
            theta = 2.0 * math.pi * ((j * f) % FINE) / FINE
            cosine, sine = np.cos(theta) / math.sqrt(FINE), np.sin(theta) / math.sqrt(FINE)
            for m in range(frames):
                w[k, 0, g, m, m, :, c, 0] = cosine
                w[k, 0, g, m, m, :, c, 1] = sine
                w[k, 1, g, m, m, :, c, 0] = -sine
                w[k, 1, g, m, m, :, c, 1] = cosine
    return w.reshape(2, 2, groups * frames, frames * FINE * COARSE * 2).astype(np.float32)


def spectra_kernel(k_ref, own_ref, other_ref, own_lead_ref, other_lead_ref, taps_ref, w_ref, real_ref, imag_ref, pad):
    first = k_ref[0] == 0
    lead = own_lead_ref.shape[0]
    lanes = own_ref.shape[1]
    for source, mate, rows in (
        (own_lead_ref, other_lead_ref, pl.ds(0, lead)),
        (own_ref, other_ref, pl.ds(lead, own_ref.shape[0])),
    ):
        a, b = source[...], mate[...]
        pad[rows, 0:lanes] = jnp.where(first, a, b)
        pad[rows, lanes : 2 * lanes] = jnp.where(first, b, a)
    frame = taps_ref.shape[1]
    chunk = w_ref.shape[3]
    per = chunk // frame
    groups = real_ref.shape[0]
    tap_rows = [jnp.concatenate([taps_ref[p], taps_ref[p]], axis=1)[None] for p in range(TAPS)]
    for part in range(own_ref.shape[0] // chunk):
        total = None
        for p in range(TAPS):
            rows = pad[pl.ds(part * chunk + (TAPS - 1 - p) * frame, chunk), :]
            term = tap_rows[p] * rows.reshape(per, frame, 2 * lanes)
            total = term if total is None else total + term
        total = total.reshape(chunk, 2 * lanes)
        for ri, goal in enumerate((real_ref, imag_ref)):
            result = jnp.dot(
                w_ref[0, ri], total, precision=lax.Precision.HIGHEST, preferred_element_type=jnp.float32
            )
            goal[:, pl.ds(part * per, per), :] = result.reshape(groups, per, 2 * lanes)


def spectra_of(k, own, other, own_lead, other_lead, taps):
    frames = 8
    rows, lanes = own.shape
    w = jnp.asarray(dft_rows(frames))
    tap_rows = jnp.broadcast_to(jnp.repeat(taps, COARSE * 2, axis=1)[:, :, None], (TAPS, FINE * COARSE * 2, lanes))
    groups = COARSE * FINE // 2
    whole = lambda shape: pl.BlockSpec(shape, lambda i, k: (0,) * len(shape))
    goal = (groups, rows // (FINE * COARSE * 2), 2 * lanes)
    return pl.pallas_call(
        spectra_kernel,
        out_shape=(jax.ShapeDtypeStruct(goal, jnp.float32),) * 2,
        grid_spec=pltpu.PrefetchScalarGridSpec(
            num_scalar_prefetch=1,
            grid=(1,),
            in_specs=[
                whole(own.shape),
                whole(other.shape),
                whole(own_lead.shape),
                whole(other_lead.shape),
                whole(tap_rows.shape),
                pl.BlockSpec((1,) + w.shape[1:], lambda i, k: (k[0], 0, 0, 0)),
            ],
            out_specs=[whole(goal)] * 2,
            scratch_shapes=[pltpu.VMEM((rows + own_lead.shape[0], 2 * lanes), jnp.float32)],
        ),
        compiler_params=pltpu.CompilerParams(vmem_limit_bytes=32 * 2**20),
    )(k, own, other, own_lead, other_lead, tap_rows, w)


E = (
    (0, 0, 0, 0),
    (4, 4, 4, 4),
    (8, 8, 8, 8),
    (5, 5, 5, 1),
    (7, 3, 3, 3),
    (1, 1, 1, 5),
    (3, 7, 7, 7),
    (6, 6, 2, 2),
    (2, 2, 6, 6),
)


def moved(block, routes):
    pairs = []
    for columns, dy, dx in routes:
        for y in range(NY):
            for x in columns:
                for core in range(2):
                    source = ((y + dy) % NY * NX + (x + dx) % NX) * 2 + core
                    pairs.append((source, (y * NX + x) * 2 + core))
    return lax.ppermute(block, "aa", pairs)


def gather(a, x, part):
    every = (0, 1, 2, 3)
    b = moved(a, [(every, 1, 0)])
    a_right = moved(a, [((0, 1, 2), 0, 1)])
    a_left = moved(a, [((0,), 0, -1)])
    d = moved(b, [(every, 2 - 1, 0)])
    b_right = moved(b, [(every, 0, 1)])
    b_left = moved(b, [(every, 0, -1)])
    if part == 0:
        from_right = moved(b_right, [((1, 2, 3), 0, 1)])
        from_left = moved(jnp.where(x == 3, b_left, d), [(every, 0, -1)])
        from_down = moved(b_right, [((3,), 1, 0)])
        far = (
            moved(jnp.where(x == 0, from_left, from_right), [((0, 1), -1, 0)]),
            moved(from_left, [((2, 3), 0, -1)]),
        )
        five, six, seven = (a_right, from_down), (from_left, a_left), (from_right, from_left)
    else:
        from_right = moved(jnp.where(x == 0, d, b_right), [((0, 3), 0, 1)])
        from_left = moved(b_left, [((1, 2, 3), 0, -1)])
        from_down = moved(b_left, [((1, 2, 3), 1, 0)])
        leaving = jnp.where(x == 1, from_left, jnp.where(x == 2, from_down, from_right))
        far = (moved(leaving, [((0, 1), -1, 0), ((2,), 0, 1), ((3,), 0, -1)]),)
        five, six, seven = (a_right, from_right), (from_down, a_left), (from_left, from_right)
    return [(a,), (b,), (d,), (b_right,), (b_left,), five, six, seven, far]


LAST = ((), (), (), (), (), (3,), (0,), (0,), (2, 3))


def split(x):
    high = x.astype(jnp.bfloat16)
    return high, (x - high.astype(jnp.float32)).astype(jnp.bfloat16)


def left_kernel(scale, real_ref, imag_ref, out_ref):
    total, width = real_ref.shape
    real, imag = split(real_ref[...].T * scale), split(imag_ref[...].T * scale)
    for part in range(2):
        out_ref[part, 0:width, 0:total] = real[part]
        out_ref[part, 0:width, total : 2 * total] = imag[part]
        out_ref[part, width : 2 * width, 0:total] = imag[part]
        out_ref[part, width : 2 * width, total : 2 * total] = -real[part]


def left_of(real, imag):
    total, width = real.shape
    return pl.pallas_call(
        functools.partial(left_kernel, 1.0 / total),
        out_shape=jax.ShapeDtypeStruct((2, 2 * width, 2 * total), jnp.bfloat16),
        compiler_params=pltpu.CompilerParams(vmem_limit_bytes=24 * 2**20),
        cost_estimate=pl.CostEstimate(flops=2 * total * width, bytes_accessed=16 * total * width, transcendentals=0),
    )(real, imag)


def correlate_kernel(columns, counts, at_ref, left_ref, *refs):
    n = len(columns)
    rights, (own_ref, send_ref), (store,) = refs[: -3], refs[-3:-1], refs[-1:]
    total, width = rights[0].shape
    half = width // 2
    first, x = at_ref[0] == 0, at_ref[1]
    place = 0
    for p in range(n):
        for part in range(2):
            count = counts[p][part]
            value = rights[place][...]
            if count == 2:
                last = functools.reduce(jnp.logical_or, [x == c for c in columns[p]])
                value = jnp.where(last, rights[place + 1][...], value)
            place += count
            high, low = split(value)
            store[p, 0, part * total : (part + 1) * total, :] = high
            store[p, 1, part * total : (part + 1) * total, :] = low

    def one(p, carry):
        dot = functools.partial(jnp.dot, preferred_element_type=jnp.float32)
        high, low = store[p, 0], store[p, 1]
        product = dot(left_ref[0], high) + dot(left_ref[0], low) + dot(left_ref[1], high)
        for r in range(2):
            for ri in range(2):
                rows0 = product[ri * width : ri * width + half, r * half : (r + 1) * half]
                rows1 = product[ri * width + half : (ri + 1) * width, r * half : (r + 1) * half]
                own_ref[2 * p + r, ri] = jnp.where(first, rows0, rows1)
                send_ref[2 * p + r, ri] = jnp.where(first, rows1, rows0)
        return carry

    lax.fori_loop(0, n, one, 0)


def correlated(at, left, positions, columns):
    n = len(positions)
    counts = tuple(tuple(len(part) for part in position) for position in positions)
    rights = [array for position in positions for part in position for array in part]
    total, width = rights[0].shape
    tiles = jax.ShapeDtypeStruct((2 * n, 2, width // 2, width // 2), jnp.float32)
    vmem = pl.BlockSpec(memory_space=pltpu.VMEM)
    return pl.pallas_call(
        functools.partial(correlate_kernel, columns, counts),
        out_shape=(tiles, tiles),
        in_specs=[pl.BlockSpec(memory_space=pltpu.SMEM)] + [vmem] * (1 + len(rights)),
        out_specs=[vmem] * 2,
        scratch_shapes=[pltpu.VMEM((n, 2, 2 * total, width), jnp.bfloat16)],
        compiler_params=pltpu.CompilerParams(vmem_limit_bytes=40 * 2**20),
        cost_estimate=pl.CostEstimate(
            flops=n * 24 * total * width * width, bytes_accessed=n * 12 * total * width, transcendentals=0
        ),
    )(at, left, *rights)


def place_kernel(sizes, at_ref, e_ref, slot_ref, *refs):
    n = len(sizes)
    owns, gots, out_ref, sems = refs[:n], refs[n : 2 * n], refs[2 * n], refs[2 * n + 1]
    k = at_ref[0]
    copies = []
    position = 0
    for own, got, size in zip(owns, gots, sizes, strict=True):
        for p in range(size):
            for r in range(2):
                distance = 2 * e_ref[position] + r - k
                unless = 1 if position == 0 and r == 0 else 0 if position == 2 and r == 1 else None
                slot = slot_ref[jnp.clip(distance, 0, slot_ref.shape[0] - 1)]
                index = 2 * (2 * position + r)
                copies.append((
                    unless,
                    pltpu.make_async_copy(own.at[2 * p + r], out_ref.at[slot, k], sems.at[index]),
                    pltpu.make_async_copy(got.at[2 * p + r], out_ref.at[slot, 1 - k], sems.at[index + 1]),
                ))
            position += 1

    def each(act):
        for unless, *pair in copies:
            if unless is None:
                for copy in pair:
                    act(copy)
            else:

                @pl.when(k != unless)
                def _(pair=pair):
                    for copy in pair:
                        act(copy)

    each(lambda copy: copy.start())
    each(lambda copy: copy.wait())


def placed(at, e, slot, owns, gots):
    half = owns[0].shape[-1]
    sizes = tuple(own.shape[0] // 2 for own in owns)
    smem, vmem = pl.BlockSpec(memory_space=pltpu.SMEM), pl.BlockSpec(memory_space=pltpu.VMEM)
    return pl.pallas_call(
        functools.partial(place_kernel, sizes),
        out_shape=jax.ShapeDtypeStruct((slot.shape[0], 2, 2, half, half), jnp.float32),
        in_specs=[smem] * 3 + [vmem] * (2 * len(owns)),
        out_specs=pl.BlockSpec(memory_space=pl.ANY),
        scratch_shapes=[pltpu.SemaphoreType.DMA((4 * sum(sizes),))],
        compiler_params=pltpu.CompilerParams(vmem_limit_bytes=24 * 2**20),
    )(at, e, slot, *owns, *gots)


GROUPS = ((0, 1), (2, 3, 4), (5, 6, 7), (8,))


def local(voltages, taps, tile_map):
    n_ta, n_aa = lax.axis_size("ta"), lax.axis_size("aa")
    me = lax.axis_index("aa").astype(jnp.int32)
    x = lax.rem(me // 2, NX)
    at = jnp.stack([lax.rem(me, 2), x])
    samples, coarse, parts, lanes = voltages.shape
    own = voltages.reshape(samples * coarse * parts, lanes)
    lead = own[own.shape[0] - (TAPS - 1) * FINE * coarse * parts :]
    mate = [(i, i ^ 1) for i in range(n_aa)]
    later = [(t * n_aa + i, (t + 1) * n_aa + i) for t in range(n_ta - 1) for i in range(n_aa)]
    own_lead = lax.ppermute(lead, ("ta", "aa"), later)
    other_lead = lax.ppermute(lead, ("ta", "aa"), [(s, d ^ 1) for s, d in later])
    other = lax.ppermute(own, "aa", mate)
    spectra = spectra_of(at, own, other, own_lead, other_lead, taps)
    blocks = [
        lax.all_to_all(part, "ta", split_axis=0, concat_axis=0, tiled=True).reshape(-1, 2 * lanes) for part in spectra
    ]
    left = left_of(*blocks)
    taken = [gather(block, x, part) for part, block in enumerate(blocks)]
    owns, gots = [], []
    for group in GROUPS:
        mine, leaving = correlated(
            at, left, [tuple(part[p] for part in taken) for p in group], tuple(LAST[p] for p in group)
        )
        owns.append(mine)
        gots.append(lax.ppermute(leaving, "aa", mate))
    slots = jnp.arange(tile_map.shape[1], dtype=jnp.int32)
    slot = jnp.sum(jnp.where(tile_map[0][None, :] == slots[:, None], slots[None, :], 0), axis=1)
    e = jnp.asarray(np.array(E, np.int32).T)[x]
    return placed(at, e, slot, owns, gots)


def solution(mesh):
    in_specs = (P("ta", None, None, "aa"), P(), P("aa", None))
    out_specs = P("aa", "ta", None, None, None)
    return jax.shard_map(local, mesh=mesh, in_specs=in_specs, out_specs=out_specs, check_vma=False)
```

```python
import functools
import math

import jax
import jax.numpy as jnp
import numpy as np
from jax import lax
from jax.experimental import pallas as pl
from jax.experimental.pallas import tpu as pltpu
from jax.sharding import PartitionSpec as P

TAPS = 4
FINE = 16
COARSE = 2
NY = 4
NX = 4


def dft_rows(frames):
    groups = COARSE * FINE // 2
    w = np.zeros((2, 2, groups, frames, frames, FINE, COARSE, 2), np.float64)
    j = np.arange(FINE)
    for k in range(2):
        for g in range(groups):
            c, f = g // (FINE // 2), 2 * (g % (FINE // 2)) + k
            theta = 2.0 * math.pi * ((j * f) % FINE) / FINE
            cosine, sine = np.cos(theta) / math.sqrt(FINE), np.sin(theta) / math.sqrt(FINE)
            for m in range(frames):
                w[k, 0, g, m, m, :, c, 0] = cosine
                w[k, 0, g, m, m, :, c, 1] = sine
                w[k, 1, g, m, m, :, c, 0] = -sine
                w[k, 1, g, m, m, :, c, 1] = cosine
    return w.reshape(2, 2, groups * frames, frames * FINE * COARSE * 2).astype(np.float32)


def spectra_kernel(k_ref, own_ref, other_ref, own_lead_ref, other_lead_ref, taps_ref, w_ref, out_ref, pad):
    first = k_ref[0] == 0
    lead = own_lead_ref.shape[0]
    lanes = own_ref.shape[1]
    for source, mate, rows in (
        (own_lead_ref, other_lead_ref, pl.ds(0, lead)),
        (own_ref, other_ref, pl.ds(lead, own_ref.shape[0])),
    ):
        a, b = source[...], mate[...]
        pad[rows, 0:lanes] = jnp.where(first, a, b)
        pad[rows, lanes : 2 * lanes] = jnp.where(first, b, a)
    frame = taps_ref.shape[1]
    chunk = w_ref.shape[3]
    per = chunk // frame
    groups = out_ref.shape[0]
    tap_rows = [jnp.concatenate([taps_ref[p], taps_ref[p]], axis=1)[None] for p in range(TAPS)]
    for part in range(own_ref.shape[0] // chunk):
        total = None
        for p in range(TAPS):
            rows = pad[pl.ds(part * chunk + (TAPS - 1 - p) * frame, chunk), :]
            term = tap_rows[p] * rows.reshape(per, frame, 2 * lanes)
            total = term if total is None else total + term
        total = total.reshape(chunk, 2 * lanes)
        for ri in range(2):
            result = jnp.dot(
                w_ref[0, ri], total, precision=lax.Precision.HIGHEST, preferred_element_type=jnp.float32
            )
            out_ref[:, pl.ds(part * per, per), pl.ds(ri * 2 * lanes, 2 * lanes)] = result.reshape(
                groups, per, 2 * lanes
            )


def spectra_of(k, own, other, own_lead, other_lead, taps):
    frames = 8
    rows, lanes = own.shape
    w = jnp.asarray(dft_rows(frames))
    tap_rows = jnp.broadcast_to(jnp.repeat(taps, COARSE * 2, axis=1)[:, :, None], (TAPS, FINE * COARSE * 2, lanes))
    groups = COARSE * FINE // 2
    whole = lambda shape: pl.BlockSpec(shape, lambda i, k: (0,) * len(shape))
    goal = (groups, rows // (FINE * COARSE * 2), 4 * lanes)
    return pl.pallas_call(
        spectra_kernel,
        out_shape=jax.ShapeDtypeStruct(goal, jnp.float32),
        grid_spec=pltpu.PrefetchScalarGridSpec(
            num_scalar_prefetch=1,
            grid=(1,),
            in_specs=[
                whole(own.shape),
                whole(other.shape),
                whole(own_lead.shape),
                whole(other_lead.shape),
                whole(tap_rows.shape),
                pl.BlockSpec((1,) + w.shape[1:], lambda i, k: (k[0], 0, 0, 0)),
            ],
            out_specs=whole(goal),
            scratch_shapes=[pltpu.VMEM((rows + own_lead.shape[0], 2 * lanes), jnp.float32)],
        ),
        compiler_params=pltpu.CompilerParams(vmem_limit_bytes=32 * 2**20),
    )(k, own, other, own_lead, other_lead, tap_rows, w)


E = (
    (0, 0, 0, 0),
    (4, 4, 4, 4),
    (8, 8, 8, 8),
    (5, 5, 5, 1),
    (7, 3, 3, 3),
    (2, 2, 2, 2),
    (1, 1, 1, 5),
    (3, 7, 7, 7),
    (6, 6, 6, 6),
)


def moved(block, routes):
    pairs = []
    for columns, dy, dx in routes:
        for y in range(NY):
            for x in columns:
                for core in range(2):
                    source = ((y + dy) % NY * NX + (x + dx) % NX) * 2 + core
                    pairs.append((source, (y * NX + x) * 2 + core))
    return lax.ppermute(block, "aa", pairs)


def gather(a, x):
    every = (0, 1, 2, 3)
    b = moved(a, [(every, 1, 0)])
    a_right = moved(a, [((0, 1, 2), 0, 1)])
    a_left = moved(a, [((0,), 0, -1)])
    b_right = moved(b, [(every, 0, 1)])
    b_left = moved(b, [(every, 0, -1)])
    d = moved(b, [(every, 1, 0)])
    from_right = moved(jnp.where((x == 1) | (x == 2), a_right, b_right), [(every, 0, 1)])
    from_left = moved(jnp.where(x == 2, d, b_left), [((0, 1, 3), 0, -1)])
    from_down = moved(jnp.where(x == 3, b_right, b_left), [((1, 2, 3), 1, 0)])
    rows = a.shape[0] // 2
    halves = pl.ds(0, rows), pl.ds(rows, rows)
    far = moved(from_down[:rows], [((2, 3), 0, -1)]), moved(from_right[rows:], [((2, 3), 1, 0)])
    both = lambda *choices: tuple(tuple((columns, array, half) for columns, array in choices) for half in halves)
    return [
        both((every, a)),
        both((every, b)),
        both((every, d)),
        both((every, b_right)),
        both((every, b_left)),
        both((every, from_right)),
        both(((0, 1, 2), a_right), ((3,), from_down)),
        both(((0,), a_left), ((1, 2), from_down), ((3,), from_left)),
        tuple((((0, 1), from_left, half), ((2, 3), last, halves[0])) for half, last in zip(halves, far, strict=True)),
    ]


def split(x):
    high = x.astype(jnp.bfloat16)
    return high, (x - high.astype(jnp.float32)).astype(jnp.bfloat16)


def left_kernel(scale, block_ref, out_ref):
    total, lanes = block_ref.shape
    width = lanes // 2
    turned = block_ref[...].T * scale
    real, imag = split(turned[:width]), split(turned[width:])
    for part in range(2):
        out_ref[part, 0:width, 0:total] = real[part]
        out_ref[part, 0:width, total : 2 * total] = imag[part]
        out_ref[part, width : 2 * width, 0:total] = imag[part]
        out_ref[part, width : 2 * width, total : 2 * total] = -real[part]


def left_of(block):
    total, lanes = block.shape
    return pl.pallas_call(
        functools.partial(left_kernel, 1.0 / total),
        out_shape=jax.ShapeDtypeStruct((2, lanes, 2 * total), jnp.bfloat16),
        compiler_params=pltpu.CompilerParams(vmem_limit_bytes=24 * 2**20),
        cost_estimate=pl.CostEstimate(flops=total * lanes, bytes_accessed=8 * total * lanes, transcendentals=0),
    )(block)


def correlate_kernel(plan, at_ref, left_ref, *refs):
    n = len(plan)
    rights, (own_ref, send_ref, store, sems) = refs[:-4], refs[-4:]
    half = own_ref.shape[-1]
    width = 2 * half
    rows = store.shape[1] // 2
    first, x = at_ref[0] == 0, at_ref[1]

    def each(p, act):
        for h, choices in enumerate(plan[p]):
            for columns, place, taken in choices:

                def one():
                    goal = store.at[p, pl.ds(h * rows, rows)]
                    act(pltpu.make_async_copy(rights[place].at[taken], goal, sems.at[2 * p + h]))

                if len(choices) == 1:
                    one()
                else:
                    pl.when(functools.reduce(jnp.logical_or, [x == c for c in columns]))(one)

    dot = functools.partial(jnp.dot, preferred_element_type=jnp.float32)
    for p in range(n):
        each(p, lambda copy: copy.start())
    for p in range(n):
        each(p, lambda copy: copy.wait())
        high, low = split(jnp.concatenate([store[p, :, :width], store[p, :, width:]], axis=0))
        product = dot(left_ref[0], high) + dot(left_ref[0], low) + dot(left_ref[1], high)
        for r in range(2):
            for ri in range(2):
                rows0 = product[ri * width : ri * width + half, r * half : (r + 1) * half]
                rows1 = product[ri * width + half : (ri + 1) * width, r * half : (r + 1) * half]
                own_ref[2 * p + r, ri] = jnp.where(first, rows0, rows1)
                send_ref[2 * p + r, ri] = jnp.where(first, rows1, rows0)


def correlated(at, left, positions):
    n = len(positions)
    arrays = []

    def place_of(array):
        for place, known in enumerate(arrays):
            if known is array:
                return place
        arrays.append(array)
        return len(arrays) - 1

    plan = [
        [[(columns, place_of(array), taken) for columns, array, taken in choices] for choices in position]
        for position in positions
    ]
    width, total = left.shape[1] // 2, left.shape[2] // 2
    tiles = jax.ShapeDtypeStruct((2 * n, 2, width // 2, width // 2), jnp.float32)
    vmem = pl.BlockSpec(memory_space=pltpu.VMEM)
    return pl.pallas_call(
        functools.partial(correlate_kernel, plan),
        out_shape=(tiles, tiles),
        in_specs=[pl.BlockSpec(memory_space=pltpu.SMEM), vmem] + [pl.BlockSpec(memory_space=pl.ANY)] * len(arrays),
        out_specs=[vmem] * 2,
        scratch_shapes=[pltpu.VMEM((n, total, 2 * width), jnp.float32), pltpu.SemaphoreType.DMA((2 * n,))],
        compiler_params=pltpu.CompilerParams(vmem_limit_bytes=40 * 2**20),
        cost_estimate=pl.CostEstimate(
            flops=n * 24 * total * width * width, bytes_accessed=n * 12 * total * width, transcendentals=0
        ),
    )(at, left, *arrays)


def place_kernel(groups, at_ref, slot_ref, *refs):
    n = len(groups)
    owns, gots, (out_ref, sems) = refs[-2 * n - 2 : -n - 2], refs[-n - 2 : -2], refs[-2:]
    k, x = at_ref[0], at_ref[1]
    copies = []
    for group, own, got in zip(groups, owns, gots, strict=True):
        for i, position in enumerate(group):
            first, *others = E[position]
            e = jnp.int32(first)
            for column, value in enumerate(others):
                if value != first:
                    e = jnp.where(x == column + 1, value, e)
            copies += tile_copies(k, position, i, e, slot_ref, own, got, out_ref, sems, len(copies))

    def each(act):
        for unless, *pair in copies:
            if unless is None:
                for copy in pair:
                    act(copy)
            else:

                @pl.when(k != unless)
                def _(pair=pair):
                    for copy in pair:
                        act(copy)

    each(lambda copy: copy.start())
    each(lambda copy: copy.wait())


def tile_copies(k, position, i, e, slot_ref, own, got, out_ref, sems, count):
    copies = []
    for r in range(2):
        distance = 2 * e + r - k
        unless = 1 if position == 0 and r == 0 else 0 if position == 2 and r == 1 else None
        slot = slot_ref[jnp.clip(distance, 0, slot_ref.shape[0] - 1)]
        tile, index = 2 * i + r, 2 * (count + r)
        copies.append((
            unless,
            pltpu.make_async_copy(own.at[tile], out_ref.at[slot, k], sems.at[index]),
            pltpu.make_async_copy(got.at[tile], out_ref.at[slot, 1 - k], sems.at[index + 1]),
        ))
    return copies


def placed(at, slot, groups, before, owns, gots):
    half = owns[0].shape[-1]
    smem, vmem = pl.BlockSpec(memory_space=pltpu.SMEM), pl.BlockSpec(memory_space=pltpu.VMEM)
    earlier = [] if before is None else [before]
    tiles = sum(own.shape[0] for own in owns)
    return pl.pallas_call(
        functools.partial(place_kernel, groups),
        out_shape=jax.ShapeDtypeStruct((slot.shape[0], 2, 2, half, half), jnp.float32),
        in_specs=[smem] * 2 + [pl.BlockSpec(memory_space=pl.ANY)] * len(earlier) + [vmem] * (2 * len(owns)),
        out_specs=pl.BlockSpec(memory_space=pl.ANY),
        input_output_aliases={2: 0} if earlier else {},
        scratch_shapes=[pltpu.SemaphoreType.DMA((2 * tiles,))],
        compiler_params=pltpu.CompilerParams(vmem_limit_bytes=24 * 2**20),
        cost_estimate=pl.CostEstimate(flops=0, bytes_accessed=16 * tiles * half * half, transcendentals=0),
    )(at, slot, *earlier, *owns, *gots)


GROUPS = ((0, 1, 2, 3, 4), (5, 6, 7), (8,))


def local(voltages, taps, tile_map):
    n_ta, n_aa = lax.axis_size("ta"), lax.axis_size("aa")
    me = lax.axis_index("aa").astype(jnp.int32)
    x = lax.rem(me // 2, NX)
    at = jnp.stack([lax.rem(me, 2), x])
    samples, coarse, parts, lanes = voltages.shape
    own = voltages.reshape(samples * coarse * parts, lanes)
    lead = own[own.shape[0] - (TAPS - 1) * FINE * coarse * parts :]
    mate = [(i, i ^ 1) for i in range(n_aa)]
    later = [(t * n_aa + i, (t + 1) * n_aa + i) for t in range(n_ta - 1) for i in range(n_aa)]
    own_lead = lax.ppermute(lead, ("ta", "aa"), later)
    other_lead = lax.ppermute(lead, ("ta", "aa"), [(s, d ^ 1) for s, d in later])
    other = lax.ppermute(own, "aa", mate)
    spectra = spectra_of(at, own, other, own_lead, other_lead, taps)
    block = lax.all_to_all(spectra, "ta", split_axis=0, concat_axis=0, tiled=True).reshape(-1, 4 * lanes)
    left = left_of(block)
    slots = jnp.arange(tile_map.shape[1], dtype=jnp.int32)
    slot = jnp.sum(jnp.where(tile_map[0][None, :] == slots[:, None], slots[None, :], 0), axis=1)
    taken = gather(block, x)
    owns, gots = [], []
    for group in GROUPS:
        mine, leaving = correlated(at, left, [taken[p] for p in group])
        owns.append(mine)
        gots.append(lax.ppermute(leaving, "aa", mate))
    return placed(at, slot, GROUPS, None, owns, gots)


def solution(mesh):
    in_specs = (P("ta", None, None, "aa"), P(), P("aa", None))
    out_specs = P("aa", "ta", None, None, None)
    return jax.shard_map(local, mesh=mesh, in_specs=in_specs, out_specs=out_specs, check_vma=False)
```

```python
import functools
import math

import jax
import jax.numpy as jnp
import numpy as np
from jax import lax
from jax.experimental import pallas as pl
from jax.experimental.pallas import tpu as pltpu
from jax.sharding import PartitionSpec as P

TAPS = 4
FINE = 16
COARSE = 2
NY = 4
NX = 4


def dft_rows(frames):
    groups = COARSE * FINE // 2
    w = np.zeros((2, 2, groups, frames, frames, FINE, COARSE, 2), np.float64)
    j = np.arange(FINE)
    for k in range(2):
        for g in range(groups):
            c, f = g // (FINE // 2), 2 * (g % (FINE // 2)) + k
            theta = 2.0 * math.pi * ((j * f) % FINE) / FINE
            cosine, sine = np.cos(theta) / math.sqrt(FINE), np.sin(theta) / math.sqrt(FINE)
            for m in range(frames):
                w[k, 0, g, m, m, :, c, 0] = cosine
                w[k, 0, g, m, m, :, c, 1] = sine
                w[k, 1, g, m, m, :, c, 0] = -sine
                w[k, 1, g, m, m, :, c, 1] = cosine
    return w.reshape(2, 2, groups * frames, frames * FINE * COARSE * 2).astype(np.float32)


def spectra_kernel(k_ref, own_ref, other_ref, own_lead_ref, other_lead_ref, taps_ref, w_ref, out_ref, pad):
    first = k_ref[0] == 0
    lead = own_lead_ref.shape[0]
    lanes = own_ref.shape[1]
    for source, mate, rows in (
        (own_lead_ref, other_lead_ref, pl.ds(0, lead)),
        (own_ref, other_ref, pl.ds(lead, own_ref.shape[0])),
    ):
        a, b = source[...], mate[...]
        pad[rows, 0:lanes] = jnp.where(first, a, b)
        pad[rows, lanes : 2 * lanes] = jnp.where(first, b, a)
    frame = taps_ref.shape[1]
    chunk = w_ref.shape[3]
    per = chunk // frame
    groups = out_ref.shape[0]
    tap_rows = [jnp.concatenate([taps_ref[p], taps_ref[p]], axis=1)[None] for p in range(TAPS)]
    for part in range(own_ref.shape[0] // chunk):
        total = None
        for p in range(TAPS):
            rows = pad[pl.ds(part * chunk + (TAPS - 1 - p) * frame, chunk), :]
            term = tap_rows[p] * rows.reshape(per, frame, 2 * lanes)
            total = term if total is None else total + term
        total = total.reshape(chunk, 2 * lanes)
        for ri in range(2):
            result = jnp.dot(
                w_ref[0, ri], total, precision=lax.Precision.HIGHEST, preferred_element_type=jnp.float32
            )
            out_ref[:, pl.ds(part * per, per), pl.ds(ri * 2 * lanes, 2 * lanes)] = result.reshape(
                groups, per, 2 * lanes
            )


def spectra_of(k, own, other, own_lead, other_lead, taps):
    frames = 8
    rows, lanes = own.shape
    w = jnp.asarray(dft_rows(frames))
    tap_rows = jnp.broadcast_to(jnp.repeat(taps, COARSE * 2, axis=1)[:, :, None], (TAPS, FINE * COARSE * 2, lanes))
    groups = COARSE * FINE // 2
    whole = lambda shape: pl.BlockSpec(shape, lambda i, k: (0,) * len(shape))
    goal = (groups, rows // (FINE * COARSE * 2), 4 * lanes)
    return pl.pallas_call(
        spectra_kernel,
        out_shape=jax.ShapeDtypeStruct(goal, jnp.float32),
        grid_spec=pltpu.PrefetchScalarGridSpec(
            num_scalar_prefetch=1,
            grid=(1,),
            in_specs=[
                whole(own.shape),
                whole(other.shape),
                whole(own_lead.shape),
                whole(other_lead.shape),
                whole(tap_rows.shape),
                pl.BlockSpec((1,) + w.shape[1:], lambda i, k: (k[0], 0, 0, 0)),
            ],
            out_specs=whole(goal),
            scratch_shapes=[pltpu.VMEM((rows + own_lead.shape[0], 2 * lanes), jnp.float32)],
        ),
        compiler_params=pltpu.CompilerParams(vmem_limit_bytes=32 * 2**20),
    )(k, own, other, own_lead, other_lead, tap_rows, w)


E = (
    (0, 0, 0, 0),
    (4, 4, 4, 4),
    (8, 8, 8, 8),
    (5, 5, 5, 1),
    (7, 3, 3, 3),
    (2, 2, 2, 2),
    (1, 1, 1, 5),
    (3, 7, 7, 7),
    (6, 6, 6, 6),
)


def moved(block, routes):
    pairs = []
    for columns, dy, dx in routes:
        for y in range(NY):
            for x in columns:
                for core in range(2):
                    source = ((y + dy) % NY * NX + (x + dx) % NX) * 2 + core
                    pairs.append((source, (y * NX + x) * 2 + core))
    return lax.ppermute(block, "aa", pairs)


def gather(a, x):
    every = (0, 1, 2, 3)
    b = moved(a, [(every, 1, 0)])
    a_right = moved(a, [((0, 1, 2), 0, 1)])
    b_right = moved(b, [(every, 0, 1)])
    b_left = moved(b, [(every, 0, -1)])
    d = moved(b, [(every, 1, 0)])
    from_right = moved(jnp.where((x == 1) | (x == 2), a_right, b_right), [(every, 0, 1)])
    from_left = moved(jnp.where((x == 1) | (x == 2), d, b_left), [(every, 0, -1)])
    from_down = moved(jnp.where(x == 3, b_right, b_left), [((1, 3), 1, 0)])
    from_up = moved(b_left, [((0,), -1, 0)])
    rows = a.shape[0] // 2
    halves = pl.ds(0, rows), pl.ds(rows, rows)
    far = moved(jnp.where(x == 2, from_left[:rows], from_down[:rows]), [((2, 3), 0, -1)]), moved(from_right[rows:], [((2, 3), 1, 0)])
    both = lambda *choices: tuple(tuple((columns, array, half) for columns, array in choices) for half in halves)
    return [
        both((every, a)),
        both((every, b)),
        both((every, d)),
        both((every, b_right)),
        both((every, b_left)),
        both((every, from_right)),
        both(((0, 1, 2), a_right), ((3,), from_down)),
        both(((0,), from_up), ((1,), from_down), ((2, 3), from_left)),
        tuple((((0, 1), from_left, half), ((2, 3), last, halves[0])) for half, last in zip(halves, far, strict=True)),
    ]


def split(x):
    high = x.astype(jnp.bfloat16)
    return high, (x - high.astype(jnp.float32)).astype(jnp.bfloat16)


def left_kernel(scale, block_ref, out_ref):
    total, lanes = block_ref.shape
    width = lanes // 2
    turned = block_ref[...].T * scale
    real, imag = split(turned[:width]), split(turned[width:])
    for part in range(2):
        out_ref[part, 0:width, 0:total] = real[part]
        out_ref[part, 0:width, total : 2 * total] = imag[part]
        out_ref[part, width : 2 * width, 0:total] = imag[part]
        out_ref[part, width : 2 * width, total : 2 * total] = -real[part]


def left_of(block):
    total, lanes = block.shape
    return pl.pallas_call(
        functools.partial(left_kernel, 1.0 / total),
        out_shape=jax.ShapeDtypeStruct((2, lanes, 2 * total), jnp.bfloat16),
        compiler_params=pltpu.CompilerParams(vmem_limit_bytes=24 * 2**20),
        cost_estimate=pl.CostEstimate(flops=total * lanes, bytes_accessed=8 * total * lanes, transcendentals=0),
    )(block)


def correlate_kernel(plan, at_ref, left_ref, *refs):
    rights, (own_ref, send_ref) = refs[:-2], refs[-2:]
    half = own_ref.shape[-1]
    width = 2 * half
    first, x = at_ref[0] == 0, at_ref[1]
    dot = functools.partial(jnp.dot, preferred_element_type=jnp.float32)
    for p, halves in enumerate(plan):
        values = []
        for choices in halves:
            _, place, taken = choices[-1]
            value = rights[place][taken, :]
            for columns, place, taken in choices[:-1]:
                here = functools.reduce(jnp.logical_or, [x == c for c in columns])
                value = jnp.where(here, rights[place][taken, :], value)
            values.append(value)
        parts = [v[:, :width] for v in values] + [v[:, width:] for v in values]
        high, low = split(jnp.concatenate(parts, axis=0))
        product = dot(left_ref[0], high) + dot(left_ref[0], low) + dot(left_ref[1], high)
        for r in range(2):
            for ri in range(2):
                rows0 = product[ri * width : ri * width + half, r * half : (r + 1) * half]
                rows1 = product[ri * width + half : (ri + 1) * width, r * half : (r + 1) * half]
                own_ref[2 * p + r, ri] = jnp.where(first, rows0, rows1)
                send_ref[2 * p + r, ri] = jnp.where(first, rows1, rows0)


def correlated(at, left, positions):
    n = len(positions)
    arrays = []

    def place_of(array):
        for place, known in enumerate(arrays):
            if known is array:
                return place
        arrays.append(array)
        return len(arrays) - 1

    plan = [
        [[(columns, place_of(array), taken) for columns, array, taken in choices] for choices in position]
        for position in positions
    ]
    width, total = left.shape[1] // 2, left.shape[2] // 2
    tiles = jax.ShapeDtypeStruct((2 * n, 2, width // 2, width // 2), jnp.float32)
    vmem = pl.BlockSpec(memory_space=pltpu.VMEM)
    return pl.pallas_call(
        functools.partial(correlate_kernel, plan),
        out_shape=(tiles, tiles),
        in_specs=[pl.BlockSpec(memory_space=pltpu.SMEM)] + [vmem] * (1 + len(arrays)),
        out_specs=[vmem] * 2,
        compiler_params=pltpu.CompilerParams(vmem_limit_bytes=20 * 2**20),
        cost_estimate=pl.CostEstimate(
            flops=n * 24 * total * width * width, bytes_accessed=n * 12 * total * width, transcendentals=0
        ),
    )(at, left, *arrays)


def place_kernel(groups, at_ref, slot_ref, *refs):
    n = len(groups)
    owns, gots, (out_ref, sems) = refs[-2 * n - 2 : -n - 2], refs[-n - 2 : -2], refs[-2:]
    k, x = at_ref[0], at_ref[1]
    copies = []
    for group, own, got in zip(groups, owns, gots, strict=True):
        for i, position in enumerate(group):
            first, *others = E[position]
            e = jnp.int32(first)
            for column, value in enumerate(others):
                if value != first:
                    e = jnp.where(x == column + 1, value, e)
            copies += tile_copies(k, position, i, e, slot_ref, own, got, out_ref, sems, len(copies))

    def each(act):
        for unless, *pair in copies:
            if unless is None:
                for copy in pair:
                    act(copy)
            else:

                @pl.when(k != unless)
                def _(pair=pair):
                    for copy in pair:
                        act(copy)

    each(lambda copy: copy.start())
    each(lambda copy: copy.wait())


def tile_copies(k, position, i, e, slot_ref, own, got, out_ref, sems, count):
    copies = []
    for r in range(2):
        distance = 2 * e + r - k
        unless = 1 if position == 0 and r == 0 else 0 if position == 2 and r == 1 else None
        slot = slot_ref[jnp.clip(distance, 0, slot_ref.shape[0] - 1)]
        tile, index = 2 * i + r, 2 * (count + r)
        copies.append((
            unless,
            pltpu.make_async_copy(own.at[tile], out_ref.at[slot, k], sems.at[index]),
            pltpu.make_async_copy(got.at[tile], out_ref.at[slot, 1 - k], sems.at[index + 1]),
        ))
    return copies


def placed(at, slot, groups, before, owns, gots):
    half = owns[0].shape[-1]
    smem, vmem = pl.BlockSpec(memory_space=pltpu.SMEM), pl.BlockSpec(memory_space=pltpu.VMEM)
    earlier = [] if before is None else [before]
    tiles = sum(own.shape[0] for own in owns)
    return pl.pallas_call(
        functools.partial(place_kernel, groups),
        out_shape=jax.ShapeDtypeStruct((slot.shape[0], 2, 2, half, half), jnp.float32),
        in_specs=[smem] * 2 + [pl.BlockSpec(memory_space=pl.ANY)] * len(earlier) + [vmem] * (2 * len(owns)),
        out_specs=pl.BlockSpec(memory_space=pl.ANY),
        input_output_aliases={2: 0} if earlier else {},
        scratch_shapes=[pltpu.SemaphoreType.DMA((2 * tiles,))],
        compiler_params=pltpu.CompilerParams(vmem_limit_bytes=24 * 2**20),
        cost_estimate=pl.CostEstimate(flops=0, bytes_accessed=16 * tiles * half * half, transcendentals=0),
    )(at, slot, *earlier, *owns, *gots)


GROUPS = ((0, 1, 2, 3, 4), (5, 6, 7, 8))


def local(voltages, taps, tile_map):
    n_ta, n_aa = lax.axis_size("ta"), lax.axis_size("aa")
    me = lax.axis_index("aa").astype(jnp.int32)
    x = lax.rem(me // 2, NX)
    at = jnp.stack([lax.rem(me, 2), x])
    samples, coarse, parts, lanes = voltages.shape
    own = voltages.reshape(samples * coarse * parts, lanes)
    lead = own[own.shape[0] - (TAPS - 1) * FINE * coarse * parts :]
    mate = [(i, i ^ 1) for i in range(n_aa)]
    later = [(t * n_aa + i, (t + 1) * n_aa + i) for t in range(n_ta - 1) for i in range(n_aa)]
    own_lead = lax.ppermute(lead, ("ta", "aa"), later)
    other_lead = lax.ppermute(lead, ("ta", "aa"), [(s, d ^ 1) for s, d in later])
    other = lax.ppermute(own, "aa", mate)
    spectra = spectra_of(at, own, other, own_lead, other_lead, taps)
    block = lax.all_to_all(spectra, "ta", split_axis=0, concat_axis=0, tiled=True).reshape(-1, 4 * lanes)
    left = left_of(block)
    slots = jnp.arange(tile_map.shape[1], dtype=jnp.int32)
    slot = jnp.sum(jnp.where(tile_map[0][None, :] == slots[:, None], slots[None, :], 0), axis=1)
    taken = gather(block, x)
    out = None
    for group in GROUPS:
        mine, leaving = correlated(at, left, [taken[p] for p in group])
        out = placed(at, slot, (group,), out, [mine], [lax.ppermute(leaving, "aa", mate)])
    return out


def solution(mesh):
    in_specs = (P("ta", None, None, "aa"), P(), P("aa", None))
    out_specs = P("aa", "ta", None, None, None)
    return jax.shard_map(local, mesh=mesh, in_specs=in_specs, out_specs=out_specs, check_vma=False)
```

```python
import functools
import math

import jax
import jax.numpy as jnp
import numpy as np
from jax import lax
from jax.experimental import pallas as pl
from jax.experimental.pallas import tpu as pltpu
from jax.sharding import PartitionSpec as P

TAPS = 4
FINE = 16
COARSE = 2
NY = 4
NX = 4


def dft_rows(frames):
    groups = COARSE * FINE // 2
    w = np.zeros((2, 2, groups, frames, frames, FINE, COARSE, 2), np.float64)
    j = np.arange(FINE)
    for k in range(2):
        for g in range(groups):
            c, f = g // (FINE // 2), 2 * (g % (FINE // 2)) + k
            theta = 2.0 * math.pi * ((j * f) % FINE) / FINE
            cosine, sine = np.cos(theta) / math.sqrt(FINE), np.sin(theta) / math.sqrt(FINE)
            for m in range(frames):
                w[k, 0, g, m, m, :, c, 0] = cosine
                w[k, 0, g, m, m, :, c, 1] = sine
                w[k, 1, g, m, m, :, c, 0] = -sine
                w[k, 1, g, m, m, :, c, 1] = cosine
    return w.reshape(2, 2, groups * frames, frames * FINE * COARSE * 2).astype(np.float32)


def spectra_kernel(k_ref, own_ref, other_ref, own_lead_ref, other_lead_ref, taps_ref, w_ref, out_ref, pad):
    first = k_ref[0] == 0
    lead = own_lead_ref.shape[0]
    lanes = own_ref.shape[1]
    for source, mate, rows in (
        (own_lead_ref, other_lead_ref, pl.ds(0, lead)),
        (own_ref, other_ref, pl.ds(lead, own_ref.shape[0])),
    ):
        a, b = source[...], mate[...]
        pad[rows, 0:lanes] = jnp.where(first, a, b)
        pad[rows, lanes : 2 * lanes] = jnp.where(first, b, a)
    frame = taps_ref.shape[1]
    chunk = w_ref.shape[3]
    per = chunk // frame
    groups = out_ref.shape[0]
    tap_rows = [jnp.concatenate([taps_ref[p], taps_ref[p]], axis=1)[None] for p in range(TAPS)]
    for part in range(own_ref.shape[0] // chunk):
        total = None
        for p in range(TAPS):
            rows = pad[pl.ds(part * chunk + (TAPS - 1 - p) * frame, chunk), :]
            term = tap_rows[p] * rows.reshape(per, frame, 2 * lanes)
            total = term if total is None else total + term
        total = total.reshape(chunk, 2 * lanes)
        for ri in range(2):
            result = jnp.dot(
                w_ref[0, ri], total, precision=lax.Precision.HIGHEST, preferred_element_type=jnp.float32
            )
            out_ref[:, pl.ds(part * per, per), pl.ds(ri * 2 * lanes, 2 * lanes)] = result.reshape(
                groups, per, 2 * lanes
            )


def spectra_of(k, own, other, own_lead, other_lead, taps):
    frames = 8
    rows, lanes = own.shape
    w = jnp.asarray(dft_rows(frames))
    tap_rows = jnp.broadcast_to(jnp.repeat(taps, COARSE * 2, axis=1)[:, :, None], (TAPS, FINE * COARSE * 2, lanes))
    groups = COARSE * FINE // 2
    whole = lambda shape: pl.BlockSpec(shape, lambda i, k: (0,) * len(shape))
    goal = (groups, rows // (FINE * COARSE * 2), 4 * lanes)
    return pl.pallas_call(
        spectra_kernel,
        out_shape=jax.ShapeDtypeStruct(goal, jnp.float32),
        grid_spec=pltpu.PrefetchScalarGridSpec(
            num_scalar_prefetch=1,
            grid=(1,),
            in_specs=[
                whole(own.shape),
                whole(other.shape),
                whole(own_lead.shape),
                whole(other_lead.shape),
                whole(tap_rows.shape),
                pl.BlockSpec((1,) + w.shape[1:], lambda i, k: (k[0], 0, 0, 0)),
            ],
            out_specs=whole(goal),
            scratch_shapes=[pltpu.VMEM((rows + own_lead.shape[0], 2 * lanes), jnp.float32)],
        ),
        compiler_params=pltpu.CompilerParams(vmem_limit_bytes=32 * 2**20),
    )(k, own, other, own_lead, other_lead, tap_rows, w)


E = (
    (0, 0, 0, 0),
    (4, 4, 4, 4),
    (8, 8, 8, 8),
    (5, 5, 5, 1),
    (7, 3, 3, 3),
    (2, 2, 2, 2),
    (1, 1, 1, 5),
    (3, 7, 7, 7),
    (6, 6, 6, 6),
)


def moved(block, routes):
    pairs = []
    for columns, dy, dx in routes:
        for y in range(NY):
            for x in columns:
                for core in range(2):
                    source = ((y + dy) % NY * NX + (x + dx) % NX) * 2 + core
                    pairs.append((source, (y * NX + x) * 2 + core))
    return lax.ppermute(block, "aa", pairs)


def gather(a, x, work):
    every = (0, 1, 2, 3)
    b = moved(a, [(every, 1, 0)])
    a_right = moved(a, [((0, 1, 2), 0, 1)])
    b_right = moved(b, [(every, 0, 1)])
    b_left = moved(b, [(every, 0, -1)])
    d = moved(b, [(every, 1, 0)])
    from_right = moved(jnp.where((x == 1) | (x == 2), a_right, b_right), [(every, 0, 1)])
    from_left = moved(jnp.where((x == 1) | (x == 2), d, b_left), [(every, 0, -1)])
    from_down = moved(jnp.where(x == 3, b_right, b_left), [((1, 3), 1, 0)])
    from_up = moved(b_left, [((0,), -1, 0)])
    rows = a.shape[0] // 2
    halves = pl.ds(0, rows), pl.ds(rows, rows)
    both = lambda *choices: tuple(tuple((columns, array, half) for columns, array in choices) for half in halves)
    near = [both((every, array)) for array in (a, b, d, b_right, b_left)]
    not_yet = jnp.minimum(jnp.abs(work(near)[0, 0, :1, :1]), 0.0) != 0.0
    far = moved(jnp.where((x == 2) | not_yet, from_left[:rows], from_down[:rows]), [((2, 3), 0, -1)]), moved(from_right[rows:], [((2, 3), 1, 0)])
    return near + [
        both((every, from_right)),
        both(((0, 1, 2), a_right), ((3,), from_down)),
        both(((0,), from_up), ((1,), from_down), ((2, 3), from_left)),
        tuple((((0, 1), from_left, half), ((2, 3), last, halves[0])) for half, last in zip(halves, far, strict=True)),
    ]


def split(x):
    high = x.astype(jnp.bfloat16)
    return high, (x - high.astype(jnp.float32)).astype(jnp.bfloat16)


def left_kernel(scale, block_ref, out_ref):
    total, lanes = block_ref.shape
    width = lanes // 2
    turned = block_ref[...].T * scale
    real, imag = split(turned[:width]), split(turned[width:])
    for part in range(2):
        out_ref[part, 0:width, 0:total] = real[part]
        out_ref[part, 0:width, total : 2 * total] = imag[part]
        out_ref[part, width : 2 * width, 0:total] = imag[part]
        out_ref[part, width : 2 * width, total : 2 * total] = -real[part]


def left_of(block):
    total, lanes = block.shape
    return pl.pallas_call(
        functools.partial(left_kernel, 1.0 / total),
        out_shape=jax.ShapeDtypeStruct((2, lanes, 2 * total), jnp.bfloat16),
        compiler_params=pltpu.CompilerParams(vmem_limit_bytes=24 * 2**20),
        cost_estimate=pl.CostEstimate(flops=total * lanes, bytes_accessed=8 * total * lanes, transcendentals=0),
    )(block)


def correlate_kernel(plan, at_ref, left_ref, *refs):
    rights, (own_ref, send_ref) = refs[:-2], refs[-2:]
    half = own_ref.shape[-1]
    width = 2 * half
    first, x = at_ref[0] == 0, at_ref[1]
    dot = functools.partial(jnp.dot, preferred_element_type=jnp.float32)
    for p, halves in enumerate(plan):
        values = []
        for choices in halves:
            _, place, taken = choices[-1]
            value = rights[place][taken, :]
            for columns, place, taken in choices[:-1]:
                here = functools.reduce(jnp.logical_or, [x == c for c in columns])
                value = jnp.where(here, rights[place][taken, :], value)
            values.append(value)
        parts = [v[:, :width] for v in values] + [v[:, width:] for v in values]
        high, low = split(jnp.concatenate(parts, axis=0))
        product = dot(left_ref[0], high) + dot(left_ref[0], low) + dot(left_ref[1], high)
        for r in range(2):
            for ri in range(2):
                rows0 = product[ri * width : ri * width + half, r * half : (r + 1) * half]
                rows1 = product[ri * width + half : (ri + 1) * width, r * half : (r + 1) * half]
                own_ref[2 * p + r, ri] = jnp.where(first, rows0, rows1)
                send_ref[2 * p + r, ri] = jnp.where(first, rows1, rows0)


def correlated(at, left, positions):
    n = len(positions)
    arrays = []

    def place_of(array):
        for place, known in enumerate(arrays):
            if known is array:
                return place
        arrays.append(array)
        return len(arrays) - 1

    plan = [
        [[(columns, place_of(array), taken) for columns, array, taken in choices] for choices in position]
        for position in positions
    ]
    width, total = left.shape[1] // 2, left.shape[2] // 2
    tiles = jax.ShapeDtypeStruct((2 * n, 2, width // 2, width // 2), jnp.float32)
    vmem = pl.BlockSpec(memory_space=pltpu.VMEM)
    return pl.pallas_call(
        functools.partial(correlate_kernel, plan),
        out_shape=(tiles, tiles),
        in_specs=[pl.BlockSpec(memory_space=pltpu.SMEM)] + [vmem] * (1 + len(arrays)),
        out_specs=[vmem] * 2,
        compiler_params=pltpu.CompilerParams(vmem_limit_bytes=20 * 2**20),
        cost_estimate=pl.CostEstimate(
            flops=n * 24 * total * width * width, bytes_accessed=n * 12 * total * width, transcendentals=0
        ),
    )(at, left, *arrays)


def place_kernel(groups, at_ref, slot_ref, *refs):
    n = len(groups)
    owns, gots, (out_ref, sems) = refs[-2 * n - 2 : -n - 2], refs[-n - 2 : -2], refs[-2:]
    k, x = at_ref[0], at_ref[1]
    copies = []
    for group, own, got in zip(groups, owns, gots, strict=True):
        for i, position in enumerate(group):
            first, *others = E[position]
            e = jnp.int32(first)
            for column, value in enumerate(others):
                if value != first:
                    e = jnp.where(x == column + 1, value, e)
            copies += tile_copies(k, position, i, e, slot_ref, own, got, out_ref, sems, len(copies))

    def each(act):
        for unless, *pair in copies:
            if unless is None:
                for copy in pair:
                    act(copy)
            else:

                @pl.when(k != unless)
                def _(pair=pair):
                    for copy in pair:
                        act(copy)

    each(lambda copy: copy.start())
    each(lambda copy: copy.wait())


def tile_copies(k, position, i, e, slot_ref, own, got, out_ref, sems, count):
    copies = []
    for r in range(2):
        distance = 2 * e + r - k
        unless = 1 if position == 0 and r == 0 else 0 if position == 2 and r == 1 else None
        slot = slot_ref[jnp.clip(distance, 0, slot_ref.shape[0] - 1)]
        tile, index = 2 * i + r, 2 * (count + r)
        copies.append((
            unless,
            pltpu.make_async_copy(own.at[tile], out_ref.at[slot, k], sems.at[index]),
            pltpu.make_async_copy(got.at[tile], out_ref.at[slot, 1 - k], sems.at[index + 1]),
        ))
    return copies


def placed(at, slot, groups, before, owns, gots):
    half = owns[0].shape[-1]
    smem, vmem = pl.BlockSpec(memory_space=pltpu.SMEM), pl.BlockSpec(memory_space=pltpu.VMEM)
    earlier = [] if before is None else [before]
    tiles = sum(own.shape[0] for own in owns)
    return pl.pallas_call(
        functools.partial(place_kernel, groups),
        out_shape=jax.ShapeDtypeStruct((slot.shape[0], 2, 2, half, half), jnp.float32),
        in_specs=[smem] * 2 + [pl.BlockSpec(memory_space=pl.ANY)] * len(earlier) + [vmem] * (2 * len(owns)),
        out_specs=pl.BlockSpec(memory_space=pl.ANY),
        input_output_aliases={2: 0} if earlier else {},
        scratch_shapes=[pltpu.SemaphoreType.DMA((2 * tiles,))],
        compiler_params=pltpu.CompilerParams(vmem_limit_bytes=24 * 2**20),
        cost_estimate=pl.CostEstimate(flops=0, bytes_accessed=16 * tiles * half * half, transcendentals=0),
    )(at, slot, *earlier, *owns, *gots)


GROUPS = ((0, 1, 2, 3, 4), (5, 6), (7, 8))


def local(voltages, taps, tile_map):
    n_ta, n_aa = lax.axis_size("ta"), lax.axis_size("aa")
    me = lax.axis_index("aa").astype(jnp.int32)
    x = lax.rem(me // 2, NX)
    at = jnp.stack([lax.rem(me, 2), x])
    samples, coarse, parts, lanes = voltages.shape
    own = voltages.reshape(samples * coarse * parts, lanes)
    lead = own[own.shape[0] - (TAPS - 1) * FINE * coarse * parts :]
    mate = [(i, i ^ 1) for i in range(n_aa)]
    later = [(t * n_aa + i, (t + 1) * n_aa + i) for t in range(n_ta - 1) for i in range(n_aa)]
    own_lead = lax.ppermute(lead, ("ta", "aa"), later)
    other_lead = lax.ppermute(lead, ("ta", "aa"), [(s, d ^ 1) for s, d in later])
    other = lax.ppermute(own, "aa", mate)
    spectra = spectra_of(at, own, other, own_lead, other_lead, taps)
    block = lax.all_to_all(spectra, "ta", split_axis=0, concat_axis=0, tiled=True).reshape(-1, 4 * lanes)
    left = left_of(block)
    slots = jnp.arange(tile_map.shape[1], dtype=jnp.int32)
    slot = jnp.sum(jnp.where(tile_map[0][None, :] == slots[:, None], slots[None, :], 0), axis=1)
    slots = jnp.arange(tile_map.shape[1], dtype=jnp.int32)
    slot = jnp.sum(jnp.where(tile_map[0][None, :] == slots[:, None], slots[None, :], 0), axis=1)
    owns, gots = [], []

    def work(positions):
        mine, leaving = correlated(at, left, positions)
        owns.append(mine)
        gots.append(lax.ppermute(leaving, "aa", mate))
        return mine

    taken = gather(block, x, work)
    for group in GROUPS[1:]:
        work([taken[p] for p in group])
    out = placed(at, slot, GROUPS[:-1], None, owns[:-1], gots[:-1])
    return placed(at, slot, GROUPS[-1:], out, owns[-1:], gots[-1:])


def solution(mesh):
    in_specs = (P("ta", None, None, "aa"), P(), P("aa", None))
    out_specs = P("aa", "ta", None, None, None)
    return jax.shard_map(local, mesh=mesh, in_specs=in_specs, out_specs=out_specs, check_vma=False)
```

```python
import functools
import math

import jax
import jax.numpy as jnp
import numpy as np
from jax import lax
from jax.experimental import pallas as pl
from jax.experimental.pallas import tpu as pltpu
from jax.sharding import PartitionSpec as P

TAPS = 4
FINE = 16
COARSE = 2
NY = 4
NX = 4


def dft_rows(frames):
    groups = COARSE * FINE // 2
    w = np.zeros((2, 2, groups, frames, frames, FINE, COARSE, 2), np.float64)
    j = np.arange(FINE)
    for k in range(2):
        for g in range(groups):
            c, f = g // (FINE // 2), 2 * (g % (FINE // 2)) + k
            theta = 2.0 * math.pi * ((j * f) % FINE) / FINE
            cosine, sine = np.cos(theta) / math.sqrt(FINE), np.sin(theta) / math.sqrt(FINE)
            for m in range(frames):
                w[k, 0, g, m, m, :, c, 0] = cosine
                w[k, 0, g, m, m, :, c, 1] = sine
                w[k, 1, g, m, m, :, c, 0] = -sine
                w[k, 1, g, m, m, :, c, 1] = cosine
    return w.reshape(2, 2, groups * frames, frames * FINE * COARSE * 2).astype(np.float32)


def spectra_kernel(k_ref, own_ref, other_ref, own_lead_ref, other_lead_ref, taps_ref, w_ref, out_ref, pad):
    first = k_ref[0] == 0
    lead = own_lead_ref.shape[0]
    lanes = own_ref.shape[1]
    for source, mate, rows in (
        (own_lead_ref, other_lead_ref, pl.ds(0, lead)),
        (own_ref, other_ref, pl.ds(lead, own_ref.shape[0])),
    ):
        a, b = source[...], mate[...]
        pad[rows, 0:lanes] = jnp.where(first, a, b)
        pad[rows, lanes : 2 * lanes] = jnp.where(first, b, a)
    frame = taps_ref.shape[1]
    chunk = w_ref.shape[3]
    per = chunk // frame
    groups = out_ref.shape[0]
    tap_rows = [jnp.concatenate([taps_ref[p], taps_ref[p]], axis=1)[None] for p in range(TAPS)]
    for part in range(own_ref.shape[0] // chunk):
        total = None
        for p in range(TAPS):
            rows = pad[pl.ds(part * chunk + (TAPS - 1 - p) * frame, chunk), :]
            term = tap_rows[p] * rows.reshape(per, frame, 2 * lanes)
            total = term if total is None else total + term
        total = total.reshape(chunk, 2 * lanes)
        for ri in range(2):
            result = jnp.dot(
                w_ref[0, ri], total, precision=lax.Precision.HIGHEST, preferred_element_type=jnp.float32
            )
            out_ref[:, pl.ds(part * per, per), pl.ds(ri * 2 * lanes, 2 * lanes)] = result.reshape(
                groups, per, 2 * lanes
            )


def spectra_of(k, own, other, own_lead, other_lead, taps):
    frames = 8
    rows, lanes = own.shape
    w = jnp.asarray(dft_rows(frames))
    tap_rows = jnp.broadcast_to(jnp.repeat(taps, COARSE * 2, axis=1)[:, :, None], (TAPS, FINE * COARSE * 2, lanes))
    groups = COARSE * FINE // 2
    whole = lambda shape: pl.BlockSpec(shape, lambda i, k: (0,) * len(shape))
    goal = (groups, rows // (FINE * COARSE * 2), 4 * lanes)
    return pl.pallas_call(
        spectra_kernel,
        out_shape=jax.ShapeDtypeStruct(goal, jnp.float32),
        grid_spec=pltpu.PrefetchScalarGridSpec(
            num_scalar_prefetch=1,
            grid=(1,),
            in_specs=[
                whole(own.shape),
                whole(other.shape),
                whole(own_lead.shape),
                whole(other_lead.shape),
                whole(tap_rows.shape),
                pl.BlockSpec((1,) + w.shape[1:], lambda i, k: (k[0], 0, 0, 0)),
            ],
            out_specs=whole(goal),
            scratch_shapes=[pltpu.VMEM((rows + own_lead.shape[0], 2 * lanes), jnp.float32)],
        ),
        compiler_params=pltpu.CompilerParams(vmem_limit_bytes=32 * 2**20),
    )(k, own, other, own_lead, other_lead, tap_rows, w)


E = (
    (0, 0, 0, 0),
    (4, 4, 4, 4),
    (8, 8, 8, 8),
    (5, 5, 5, 1),
    (7, 3, 3, 3),
    (2, 2, 2, 2),
    (1, 1, 1, 5),
    (3, 7, 7, 7),
    (6, 6, 6, 6),
)


def moved(block, routes):
    pairs = []
    for columns, dy, dx in routes:
        for y in range(NY):
            for x in columns:
                for core in range(2):
                    source = ((y + dy) % NY * NX + (x + dx) % NX) * 2 + core
                    pairs.append((source, (y * NX + x) * 2 + core))
    return lax.ppermute(block, "aa", pairs)


def gather(a, x, work):
    every = (0, 1, 2, 3)
    b = moved(a, [(every, 1, 0)])
    a_right = moved(a, [((0, 1, 2), 0, 1)])
    b_right = moved(b, [(every, 0, 1)])
    b_left = moved(b, [(every, 0, -1)])
    d = moved(b, [(every, 1, 0)])
    from_right = moved(jnp.where((x == 1) | (x == 2), a_right, b_right), [(every, 0, 1)])
    from_left = moved(jnp.where((x == 1) | (x == 2), d, b_left), [(every, 0, -1)])
    from_down = moved(jnp.where(x == 3, b_right, b_left), [((1, 3), 1, 0)])
    from_up = moved(b_left, [((0,), -1, 0)])
    rows = a.shape[0] // 2
    halves = pl.ds(0, rows), pl.ds(rows, rows)
    both = lambda *choices: tuple(tuple((columns, array, half) for columns, array in choices) for half in halves)
    near = [both((every, array)) for array in (a, b, d, b_right, b_left)]
    not_yet = jnp.minimum(jnp.abs(work(near)[0, 0, :1, :1]), 0.0) != 0.0
    far = moved(jnp.where((x == 2) | not_yet, from_left[:rows], from_down[:rows]), [((2, 3), 0, -1)]), moved(from_right[rows:], [((2, 3), 1, 0)])
    return near + [
        both((every, from_right)),
        both(((0, 1, 2), a_right), ((3,), from_down)),
        both(((0,), from_up), ((1,), from_down), ((2, 3), from_left)),
        tuple((((0, 1), from_left, half), ((2, 3), last, halves[0])) for half, last in zip(halves, far, strict=True)),
    ]


def split(x):
    high = x.astype(jnp.bfloat16)
    return high, (x - high.astype(jnp.float32)).astype(jnp.bfloat16)


def left_kernel(scale, block_ref, out_ref):
    total, lanes = block_ref.shape
    width = lanes // 2
    turned = block_ref[...].T * scale
    real, imag = split(turned[:width]), split(turned[width:])
    for part in range(2):
        out_ref[part, 0:width, 0:total] = real[part]
        out_ref[part, 0:width, total : 2 * total] = imag[part]
        out_ref[part, width : 2 * width, 0:total] = imag[part]
        out_ref[part, width : 2 * width, total : 2 * total] = -real[part]


def left_of(block):
    total, lanes = block.shape
    return pl.pallas_call(
        functools.partial(left_kernel, 1.0 / total),
        out_shape=jax.ShapeDtypeStruct((2, lanes, 2 * total), jnp.bfloat16),
        compiler_params=pltpu.CompilerParams(vmem_limit_bytes=24 * 2**20),
        cost_estimate=pl.CostEstimate(flops=total * lanes, bytes_accessed=8 * total * lanes, transcendentals=0),
    )(block)


def correlate_kernel(plan, at_ref, left_ref, *refs):
    rights, (own_ref, send_ref) = refs[:-2], refs[-2:]
    half = own_ref.shape[-1]
    width = 2 * half
    first, x = at_ref[0] == 0, at_ref[1]
    dot = functools.partial(jnp.dot, preferred_element_type=jnp.float32)
    for p, halves in enumerate(plan):
        values = []
        for choices in halves:
            _, place, taken = choices[-1]
            value = rights[place][taken, :]
            for columns, place, taken in choices[:-1]:
                here = functools.reduce(jnp.logical_or, [x == c for c in columns])
                value = jnp.where(here, rights[place][taken, :], value)
            values.append(value)
        parts = [v[:, :width] for v in values] + [v[:, width:] for v in values]
        high, low = split(jnp.concatenate(parts, axis=0))
        product = dot(left_ref[0], high) + dot(left_ref[0], low) + dot(left_ref[1], high)
        for r in range(2):
            for ri in range(2):
                rows0 = product[ri * width : ri * width + half, r * half : (r + 1) * half]
                rows1 = product[ri * width + half : (ri + 1) * width, r * half : (r + 1) * half]
                own_ref[2 * p + r, ri] = jnp.where(first, rows0, rows1)
                send_ref[2 * p + r, ri] = jnp.where(first, rows1, rows0)


def correlated(at, left, positions):
    n = len(positions)
    arrays = []

    def place_of(array):
        for place, known in enumerate(arrays):
            if known is array:
                return place
        arrays.append(array)
        return len(arrays) - 1

    plan = [
        [[(columns, place_of(array), taken) for columns, array, taken in choices] for choices in position]
        for position in positions
    ]
    width, total = left.shape[1] // 2, left.shape[2] // 2
    tiles = jax.ShapeDtypeStruct((2 * n, 2, width // 2, width // 2), jnp.float32)
    vmem = pl.BlockSpec(memory_space=pltpu.VMEM)
    return pl.pallas_call(
        functools.partial(correlate_kernel, plan),
        out_shape=(tiles, tiles),
        in_specs=[pl.BlockSpec(memory_space=pltpu.SMEM)] + [vmem] * (1 + len(arrays)),
        out_specs=[vmem] * 2,
        compiler_params=pltpu.CompilerParams(vmem_limit_bytes=20 * 2**20),
        cost_estimate=pl.CostEstimate(
            flops=n * 24 * total * width * width, bytes_accessed=n * 12 * total * width, transcendentals=0
        ),
    )(at, left, *arrays)


def place_kernel(groups, at_ref, slot_ref, *refs):
    n = len(groups)
    owns, gots, (out_ref, sems) = refs[-2 * n - 2 : -n - 2], refs[-n - 2 : -2], refs[-2:]
    k, x = at_ref[0], at_ref[1]
    copies = []
    for group, own, got in zip(groups, owns, gots, strict=True):
        for i, position in enumerate(group):
            first, *others = E[position]
            e = jnp.int32(first)
            for column, value in enumerate(others):
                if value != first:
                    e = jnp.where(x == column + 1, value, e)
            copies += tile_copies(k, position, i, e, slot_ref, own, got, out_ref, sems, len(copies))

    def each(act):
        for unless, *pair in copies:
            if unless is None:
                for copy in pair:
                    act(copy)
            else:

                @pl.when(k != unless)
                def _(pair=pair):
                    for copy in pair:
                        act(copy)

    each(lambda copy: copy.start())
    each(lambda copy: copy.wait())


def tile_copies(k, position, i, e, slot_ref, own, got, out_ref, sems, count):
    copies = []
    for r in range(2):
        distance = 2 * e + r - k
        unless = 1 if position == 0 and r == 0 else 0 if position == 2 and r == 1 else None
        slot = slot_ref[jnp.clip(distance, 0, slot_ref.shape[0] - 1)]
        tile, index = 2 * i + r, 2 * (count + r)
        copies.append((
            unless,
            pltpu.make_async_copy(own.at[tile], out_ref.at[slot, k], sems.at[index]),
            pltpu.make_async_copy(got.at[tile], out_ref.at[slot, 1 - k], sems.at[index + 1]),
        ))
    return copies


def placed(at, slot, groups, before, owns, gots):
    half = owns[0].shape[-1]
    smem, vmem = pl.BlockSpec(memory_space=pltpu.SMEM), pl.BlockSpec(memory_space=pltpu.VMEM)
    earlier = [] if before is None else [before]
    tiles = sum(own.shape[0] for own in owns)
    return pl.pallas_call(
        functools.partial(place_kernel, groups),
        out_shape=jax.ShapeDtypeStruct((slot.shape[0], 2, 2, half, half), jnp.float32),
        in_specs=[smem] * 2 + [pl.BlockSpec(memory_space=pl.ANY)] * len(earlier) + [vmem] * (2 * len(owns)),
        out_specs=pl.BlockSpec(memory_space=pl.ANY),
        input_output_aliases={2: 0} if earlier else {},
        scratch_shapes=[pltpu.SemaphoreType.DMA((2 * tiles,))],
        compiler_params=pltpu.CompilerParams(vmem_limit_bytes=24 * 2**20),
        cost_estimate=pl.CostEstimate(flops=0, bytes_accessed=16 * tiles * half * half, transcendentals=0),
    )(at, slot, *earlier, *owns, *gots)


GROUPS = ((0, 1, 2, 3, 4), (5, 6), (7, 8))


def local(voltages, taps, tile_map):
    n_ta, n_aa = lax.axis_size("ta"), lax.axis_size("aa")
    me = lax.axis_index("aa").astype(jnp.int32)
    x = lax.rem(me // 2, NX)
    at = jnp.stack([lax.rem(me, 2), x])
    samples, coarse, parts, lanes = voltages.shape
    own = voltages.reshape(samples * coarse * parts, lanes)
    lead = own[own.shape[0] - (TAPS - 1) * FINE * coarse * parts :]
    mate = [(i, i ^ 1) for i in range(n_aa)]
    later = [(t * n_aa + i, (t + 1) * n_aa + i) for t in range(n_ta - 1) for i in range(n_aa)]
    own_lead = lax.ppermute(lead, ("ta", "aa"), later)
    other_lead = lax.ppermute(own_lead, "aa", mate)
    other = lax.ppermute(own, "aa", mate)
    spectra = spectra_of(at, own, other, own_lead, other_lead, taps)
    block = lax.all_to_all(spectra, "ta", split_axis=0, concat_axis=0, tiled=True).reshape(-1, 4 * lanes)
    left = left_of(block)
    slots = jnp.arange(tile_map.shape[1], dtype=jnp.int32)
    slot = jnp.sum(jnp.where(tile_map[0][None, :] == slots[:, None], slots[None, :], 0), axis=1)
    slots = jnp.arange(tile_map.shape[1], dtype=jnp.int32)
    slot = jnp.sum(jnp.where(tile_map[0][None, :] == slots[:, None], slots[None, :], 0), axis=1)
    owns, gots = [], []

    def work(positions):
        mine, leaving = correlated(at, left, positions)
        owns.append(mine)
        gots.append(lax.ppermute(leaving, "aa", mate))
        return mine

    taken = gather(block, x, work)
    for group in GROUPS[1:]:
        work([taken[p] for p in group])
    out = placed(at, slot, GROUPS[:-1], None, owns[:-1], gots[:-1])
    return placed(at, slot, GROUPS[-1:], out, owns[-1:], gots[-1:])


def solution(mesh):
    in_specs = (P("ta", None, None, "aa"), P(), P("aa", None))
    out_specs = P("aa", "ta", None, None, None)
    return jax.shard_map(local, mesh=mesh, in_specs=in_specs, out_specs=out_specs, check_vma=False)
```
